128 devices in a mesh: replica: 8 (over y_hi, z), tensor: 16 (over x, y_lo, core).
Axes of the slice: x: 4, y: 4 (y_hi: 2, y_lo: 2; y = y_hi * 2 + y_lo), z: 4, core: 2. Of those that a mesh axis runs over, the one named last changes fastest.
Arguments:
- query_codes: bfloat16 [2, 1536, 128, 128], P(None, ('replica', 'tensor')), may hold values from -4 to 4
- key_codes: bfloat16 [2, 512, 128, 128], P(None, ('replica', 'tensor')), may hold values from -4 to 4
- query_scales: float32 [2, 12, 128], P(None, None, 'tensor'), may hold values from 0.25 to 4
- key_scales: float32 [2, 4, 128], P(None, None, 'tensor'), may hold values from 0.25 to 4
Outputs:
- absorbed: bfloat16 [2, 128, 1536, 512], P(None, 'tensor')
- block_scale: float32 [2, 128, 12, 4], P(None, 'tensor')
The draws below stay inside these ranges and needn't reach their ends.
All inputs are finite; a program needn't handle non-finite values. Where the reference program divides by a largest or mean magnitude, that divisor is 1e-20 or more.
Results may differ from the reference program's by a relative error of at most 0.006.
Values may be sent and summed in bfloat16 or wider, within the bound.
No kernel may reach another device: no remote copies, remote signals or barrier semaphores. Data moves between devices by JAX's collectives and lax.ppermute only.
A program may use at most 320 MiB of HBM per device.

```python
import math
import jax
import jax.numpy as jnp
from jax import lax

QR = 1536
KVR = 512
HEADS = 128
HD = 128
BLK = 128
LAYERS = 2


def level_of(rng, extent, split, low, largest):
    factor_of = 1.0
    for position, parts in split:
        draws = jax.random.uniform(jax.random.fold_in(jax.random.fold_in(rng, 6), position), (parts,), jnp.float32, low / len(split), largest / len(split))
        factor_of = factor_of * jnp.repeat(jnp.exp(draws), extent[position] // parts).reshape((-1,) + (1,) * (len(extent) - 1 - position))
    return factor_of


def bell_draw(key, extent, scale, most, shards=(), held_as=jnp.bfloat16):
    values = scale * jax.random.normal(key, extent, jnp.float32)
    if shards:
        values = values * level_of(key, extent, shards, -0.22, 0.18)
    return jnp.clip(values, -most, most).astype(held_as)


def setup_inputs(seed: int = 0) -> dict:
    splits = jax.random.split(jax.random.key(seed), 5)
    return {
        "query_codes": bell_draw(splits[0], (LAYERS, QR, HEADS, HD), 0.25, 4.0, ((1, 128),)),
        "key_codes": bell_draw(splits[1], (LAYERS, KVR, HEADS, HD), 0.25, 4.0, ((1, 128),)),
        "query_scales": jnp.clip(jnp.exp(math.log(4.0) - 2.7725887 * jax.random.uniform(splits[2], (LAYERS, QR // BLK, HEADS), jnp.float32) ** level_of(splits[2], (LAYERS, QR // BLK, HEADS), ((2, 16),), -0.2, 0.2)), 0.25, 4.0),
        "key_scales": jnp.clip(jnp.exp(math.log(4.0) - 2.7725887 * jax.random.uniform(splits[3], (LAYERS, KVR // BLK, HEADS), jnp.float32) ** level_of(splits[3], (LAYERS, KVR // BLK, HEADS), ((2, 16),), -0.2, 0.2)), 0.25, 4.0),
    }


eps = 1e-6


def one_head(items):
    query_rows, key_rows, query_scale, key_scale = items
    query_weight = (query_rows.astype(jnp.float32).reshape(QR // BLK, BLK, HD) * query_scale[:, None, None]).reshape(QR, HD).astype(jnp.bfloat16)
    key_weight = (key_rows.astype(jnp.float32).reshape(KVR // BLK, BLK, HD) * key_scale[:, None, None]).reshape(KVR, HD).astype(jnp.bfloat16)
    product = jnp.dot(query_weight, key_weight.T, preferred_element_type=jnp.float32)
    blocks = product.reshape(QR // BLK, BLK, KVR // BLK, BLK)
    peak = jnp.max(jnp.abs(blocks), axis=(1, 3)) + eps
    scaled = (blocks / peak[:, None, :, None]).reshape(QR, KVR).astype(jnp.bfloat16)
    return scaled, peak


def reference(query_codes, key_codes, query_scales, key_scales):
    absorbed_list = []
    scale_list = []
    for layer in range(LAYERS):
        items = (jnp.moveaxis(query_codes[layer], 1, 0), jnp.moveaxis(key_codes[layer], 1, 0), query_scales[layer].T, key_scales[layer].T)
        scaled, peak = lax.map(one_head, items)
        absorbed_list.append(scaled)
        scale_list.append(peak)
    return jnp.stack(absorbed_list), jnp.stack(scale_list)
```

```python
import functools

import jax
import jax.numpy as jnp
import numpy as np
from jax import lax
from jax.experimental import pallas as pl
from jax.experimental.pallas import tpu as pltpu
from jax.sharding import PartitionSpec as P

BLK = 128
EPS = 1e-06
REPLICAS = 8
QROWS = 192
KROWS = 64
ROWS = QROWS + KROWS


def regroup_matrix():
    matrix = np.zeros((512, 512), np.float32)
    for source in range(4):
        for row in range(16):
            for head in range(8):
                if row < 12:
                    to = head * 64 + source * 12 + row
                else:
                    to = head * 64 + 48 + source * 4 + (row - 12)
                matrix[to, source * 128 + row * 8 + head] = 1.0
    return matrix


def regroup_kernel(matrix_ref, dealt_ref, out_ref):
    for group in range(4):
        rows = dealt_ref[4 * group : 4 * group + 4, 0].reshape(512, 128)
        moved = jnp.dot(matrix_ref[...], rows, preferred_element_type=jnp.float32).astype(jnp.bfloat16)
        for head in range(8):
            out_ref[0, head, 48 * group : 48 * group + 48] = moved[64 * head : 64 * head + 48]
            out_ref[0, head, QROWS + 16 * group : QROWS + 16 * group + 16] = moved[64 * head + 48 : 64 * head + 64]


def regroup(dealt):
    layers = dealt.shape[1]
    matrix = jnp.asarray(regroup_matrix(), jnp.bfloat16)
    return pl.pallas_call(
        regroup_kernel,
        grid=(layers,),
        in_specs=[
            pl.BlockSpec((512, 512), lambda l: (0, 0)),
            pl.BlockSpec((16, 1, 128, 128), lambda l: (0, l, 0, 0)),
        ],
        out_specs=pl.BlockSpec((1, 8, ROWS, 128), lambda l: (l, 0, 0, 0)),
        out_shape=jax.ShapeDtypeStruct((layers, 8, ROWS, 128), jnp.bfloat16),
        compiler_params=pltpu.CompilerParams(vmem_limit_bytes=32 * 2**20),
        name="regroup",
    )(matrix, dealt)


def absorb_kernel(query_scales_ref, key_scales_ref, *refs):
    pieces, (out_ref, scale_ref, query_ref, key_ref) = refs[:-4], refs[-4:]
    layer, head = pl.program_id(0), pl.program_id(1)
    for place, piece in enumerate(pieces):
        query_ref[QROWS * place : QROWS * (place + 1)] = piece[0, 0, 0, :QROWS]
        key_ref[KROWS * place : KROWS * (place + 1)] = piece[0, 0, 0, QROWS:]
    for i in range(12):
        dots = lax.dot_general(
            query_ref[BLK * i : BLK * (i + 1)], key_ref[...], (((1,), (1,)), ((), ())), preferred_element_type=jnp.float32
        )
        for j in range(4):
            block = dots[:, BLK * j : BLK * (j + 1)]
            factor = query_scales_ref[layer, i, head] * key_scales_ref[layer, j, head]
            peak = jnp.max(jnp.abs(block), axis=(0, 1), keepdims=True) * factor + EPS
            scale_ref[0, 0, i : i + 1, j : j + 1] = peak
            out_ref[0, 0, BLK * i : BLK * (i + 1), BLK * j : BLK * (j + 1)] = (block * (factor / peak)).astype(jnp.bfloat16)


def absorb(query_scales, key_scales, gathered):
    return pl.pallas_call(
        absorb_kernel,
        grid=(2, 8),
        in_specs=[
            pl.BlockSpec(memory_space=pltpu.SMEM),
            pl.BlockSpec(memory_space=pltpu.SMEM),
        ]
        + [pl.BlockSpec((1, 1, 1, ROWS, 128), lambda l, h, r=r: (r, l, h, 0, 0)) for r in range(REPLICAS)],
        out_specs=[
            pl.BlockSpec((1, 1, 1536, 512), lambda l, h: (l, h, 0, 0)),
            pl.BlockSpec((1, 1, 12, 4), lambda l, h: (l, h, 0, 0)),
        ],
        out_shape=[
            jax.ShapeDtypeStruct((2, 8, 1536, 512), jnp.bfloat16),
            jax.ShapeDtypeStruct((2, 8, 12, 4), jnp.float32),
        ],
        scratch_shapes=[pltpu.VMEM((1536, 128), jnp.bfloat16), pltpu.VMEM((512, 128), jnp.bfloat16)],
        compiler_params=pltpu.CompilerParams(vmem_limit_bytes=40 * 2**20),
        name="absorb",
    )(query_scales, key_scales, *([gathered] * REPLICAS))


def local(query_codes, key_codes, query_scales, key_scales):
    parted = [
        codes.reshape(2, codes.shape[1], 16, 8, 128).transpose(2, 0, 1, 3, 4) for codes in (query_codes, key_codes)
    ]
    sent = jnp.concatenate(parted, axis=2).reshape(16, 2, 128, 128)
    dealt = lax.all_to_all(sent, "tensor", split_axis=0, concat_axis=0, tiled=True)
    own = regroup(dealt)
    gathered = lax.all_gather(own, "replica", axis=0, tiled=False)
    return tuple(absorb(query_scales, key_scales, gathered))


def solution(mesh):
    return jax.shard_map(
        local,
        mesh=mesh,
        in_specs=(
            P(None, ("replica", "tensor"), None, None),
            P(None, ("replica", "tensor"), None, None),
            P(None, None, "tensor"),
            P(None, None, "tensor"),
        ),
        out_specs=(P(None, "tensor", None, None), P(None, "tensor", None, None)),
        check_vma=False,
    )
```

```python
import functools

import jax
import jax.numpy as jnp
from jax import lax
from jax.experimental import pallas as pl
from jax.experimental.pallas import tpu as pltpu
from jax.sharding import PartitionSpec as P

BLK = 128
EPS = 1e-06
QROWS = 192
KROWS = 64
ROWS = QROWS + KROWS
Z = 4
Y = 2
HEADS = 8
UNITS = 2 * HEADS
PARTS = ((0, 9), (9, 16))
PIECES = ((0, 0), (1, 0), (0, -1), (0, 1), (0, 2), (1, -1), (1, 1), (1, 2))


def prepare_kernel(query_hbm, key_hbm, query_scales_hbm, key_scales_hbm, sent_ref, scales_ref, query_ref, key_ref, query_scales_ref, key_scales_ref, semaphores):
    moves = [
        pltpu.make_async_copy(source, to, semaphores.at[n])
        for n, (source, to) in enumerate(
            ((query_hbm, query_ref), (key_hbm, key_ref), (query_scales_hbm, query_scales_ref), (key_scales_hbm, key_scales_ref))
        )
    ]
    for move in moves:
        move.start()
    for move in moves:
        move.wait()
    for to in range(16):
        for layer in range(2):
            for rows_ref, start in ((query_ref, 0), (key_ref, 12)):
                rows = rows_ref.shape[1]
                tiles = rows_ref[layer, :, 8 * to : 8 * to + 8].reshape(8 * rows, 128)
                sent_ref[to, layer, 8 * start : 8 * (start + rows)] = tiles
    scales_ref[:, :12] = query_scales_ref[...].transpose(0, 2, 1)
    scales_ref[:, 12:] = key_scales_ref[...]


def prepare(query_codes, key_codes, query_scales, key_scales):
    args = (query_codes, key_codes, query_scales.transpose(0, 2, 1), key_scales)
    return pl.pallas_call(
        prepare_kernel,
        in_specs=[pl.BlockSpec(memory_space=pltpu.HBM)] * 4,
        out_specs=[pl.BlockSpec(memory_space=pltpu.VMEM)] * 2,
        out_shape=[
            jax.ShapeDtypeStruct((16, 2, 128, 128), jnp.bfloat16),
            jax.ShapeDtypeStruct((2, 16, 8), jnp.float32),
        ],
        scratch_shapes=[pltpu.VMEM(x.shape, x.dtype) for x in args] + [pltpu.SemaphoreType.DMA((4,))],
        compiler_params=pltpu.CompilerParams(vmem_limit_bytes=60 * 2**20),
        name="prepare",
    )(*args)


def regroup_matrix():
    to = lax.broadcasted_iota(jnp.int32, (256, 256), 0)
    head, place = to // 32, to % 32
    query = place < 24
    source = jnp.where(query, place // 12, (place - 24) // 4)
    row = jnp.where(query, place % 12, 12 + place % 4)
    start = source * 128 + row * 8 + head
    return (lax.broadcasted_iota(jnp.int32, (256, 256), 1) == start).astype(jnp.bfloat16)


def regroup_kernel(device_ref, scales_ref, dealt_ref, *out_refs):
    replica = device_ref[0] // 16
    matrix = regroup_matrix()
    for layer in range(2):
        codes = []
        for pair in range(8):
            rows = dealt_ref[2 * pair : 2 * pair + 2, layer].reshape(256, 128)
            codes.append(jnp.dot(matrix, rows, preferred_element_type=jnp.float32))
        for head in range(HEADS):
            unit = layer * HEADS + head
            out_ref, at = next((ref, unit - start) for ref, (start, end) in zip(out_refs, PARTS) if start <= unit < end)
            query = jnp.concatenate([c[32 * head : 32 * head + 24] for c in codes])
            for part in range(3):
                scale = scales_ref[layer, (3 * replica + part) // 2, head]
                out_ref[at, 64 * part : 64 * part + 64] = (query[64 * part : 64 * part + 64] * scale).astype(jnp.bfloat16)
            key = jnp.concatenate([c[32 * head + 24 : 32 * head + 32] for c in codes])
            scale = scales_ref[layer, 12 + replica // 2, head]
            out_ref[at, QROWS:] = (key * scale).astype(jnp.bfloat16)


def regroup(device, scales, dealt):
    smem, vmem = pl.BlockSpec(memory_space=pltpu.SMEM), pl.BlockSpec(memory_space=pltpu.VMEM)
    return pl.pallas_call(
        regroup_kernel,
        in_specs=[smem, smem, vmem],
        out_specs=[vmem] * len(PARTS),
        out_shape=[jax.ShapeDtypeStruct((end - start, ROWS, 128), jnp.bfloat16) for start, end in PARTS],
        compiler_params=pltpu.CompilerParams(vmem_limit_bytes=8 * 2**20),
        name="regroup",
    )(device, scales, dealt)


def absorb_kernel(device_ref, *refs):
    pieces, (out_ref, scale_ref, query_ref, key_ref) = refs[: len(PIECES)], refs[-4:]
    replica, core = device_ref[0] // 16, device_ref[0] % 2
    y, z, spin = replica // Z, replica % Z, 1 - 2 * core
    for (dy, dz), piece in zip(PIECES, pieces):
        place = (y + dy) % Y * Z + (z + Z + dz * spin) % Z
        query_ref[pl.ds(pl.multiple_of(QROWS * place, QROWS), QROWS)] = piece[0, :QROWS]
        key_ref[pl.ds(pl.multiple_of(KROWS * place, KROWS), KROWS)] = piece[0, QROWS:]
    for i in range(12):
        dots = lax.dot_general(
            query_ref[BLK * i : BLK * (i + 1)], key_ref[...], (((1,), (1,)), ((), ())), preferred_element_type=jnp.float32
        )
        for j in range(4):
            block = dots[:, BLK * j : BLK * (j + 1)]
            peak = jnp.max(jnp.abs(block), axis=(0, 1), keepdims=True) + EPS
            scale_ref[0, 0, j : j + 1, i : i + 1] = peak
            out_ref[0, 0, BLK * i : BLK * (i + 1), BLK * j : BLK * (j + 1)] = (block * (1.0 / peak)).astype(jnp.bfloat16)


def absorb(device, part, pieces, outs):
    any_space = pl.BlockSpec(memory_space=pl.ANY)
    earlier = () if outs is None else tuple(outs)
    start, end = part
    return pl.pallas_call(
        absorb_kernel,
        grid_spec=pltpu.PrefetchScalarGridSpec(
            num_scalar_prefetch=1,
            grid=(end - start,),
            in_specs=[pl.BlockSpec((1, ROWS, 128), lambda u, device: (u, 0, 0))] * len(PIECES) + [any_space] * len(earlier),
            out_specs=[
                pl.BlockSpec((1, 1, 1536, 512), lambda u, device: ((start + u) // HEADS, (start + u) % HEADS, 0, 0)),
                pl.BlockSpec((1, 1, 4, 12), lambda u, device: ((start + u) // HEADS, (start + u) % HEADS, 0, 0)),
            ],
            scratch_shapes=[pltpu.VMEM((1536, 128), jnp.bfloat16), pltpu.VMEM((512, 128), jnp.bfloat16)],
        ),
        out_shape=[
            jax.ShapeDtypeStruct((2, HEADS, 1536, 512), jnp.bfloat16),
            jax.ShapeDtypeStruct((2, HEADS, 4, 12), jnp.float32),
        ],
        input_output_aliases={1 + len(pieces) + n: n for n in range(len(earlier))},
        compiler_params=pltpu.CompilerParams(vmem_limit_bytes=14 * 2**20),
        cost_estimate=pl.CostEstimate(flops=1, bytes_accessed=1, transcendentals=0),
        name="absorb",
    )(device, *pieces, *earlier)


def along_z(x, step):
    def to(replica, tensor):
        spin = 1 - 2 * (tensor % 2)
        return replica // Z * Z + (replica + step * spin) % Z

    pairs = [(16 * r + t, 16 * to(r, t) + t) for r in range(Y * Z) for t in range(16)]
    return lax.ppermute(x, ("replica", "tensor"), pairs)


def across_y(x):
    return lax.ppermute(x, "replica", [(y * Z + z, (1 - y) * Z + z) for y in range(Y) for z in range(Z)])


def together(*arrays):
    return lax.optimization_barrier(arrays)


def local(query_codes, key_codes, query_scales, key_scales):
    device = lax.axis_index(("replica", "tensor")).astype(jnp.int32).reshape(1)
    sent, scales = prepare(query_codes, key_codes, query_scales, key_scales)
    dealt = lax.all_to_all(sent, "tensor", split_axis=0, concat_axis=0, tiled=True)
    first, second = regroup(device, scales, dealt)

    over_2 = across_y(second)
    over_behind_2 = along_z(over_2, 1)
    behind = along_z(first, 1)
    behind_2 = along_z(second, 1)
    far_2 = along_z(behind_2, 1)
    far = along_z(behind, 1)
    over = across_y(first)
    over, behind_2 = together(over, behind_2)
    ahead_2 = along_z(second, -1)
    ahead = along_z(first, -1)
    over_behind = along_z(over, 1)
    over_behind, ahead_2 = together(over_behind, ahead_2)
    over_behind, over_2 = together(over_behind, over_2)
    over_far = along_z(over_behind, 1)
    over_far_2 = along_z(over_behind_2, 1)
    over_ahead_2 = across_y(ahead_2)
    over_ahead = across_y(ahead)

    outs = absorb(device, PARTS[0], (first, over, behind, ahead, far, over_behind, over_ahead, over_far), None)
    pieces = (second, over_2, behind_2, ahead_2, far_2, over_behind_2, over_ahead_2, over_far_2)
    outs = absorb(device, PARTS[1], pieces, outs)
    return outs[0], outs[1].transpose(0, 1, 3, 2)


def solution(mesh):
    return jax.shard_map(
        local,
        mesh=mesh,
        in_specs=(
            P(None, ("replica", "tensor"), None, None),
            P(None, ("replica", "tensor"), None, None),
            P(None, None, "tensor"),
            P(None, None, "tensor"),
        ),
        out_specs=(P(None, "tensor", None, None), P(None, "tensor", None, None)),
        check_vma=False,
    )
```

```python
import functools

import jax
import jax.numpy as jnp
from jax import lax
from jax.experimental import pallas as pl
from jax.experimental.pallas import tpu as pltpu
from jax.sharding import PartitionSpec as P

BLK = 128
EPS = 1e-06
QROWS = 192
KROWS = 64
ROWS = QROWS + KROWS
Z = 4
Y = 2
HEADS = 8
UNITS = 2 * HEADS
PARTS = ((0, 10), (10, 16))
PIECES = ((0, 0), (0, -1), (0, -2), (0, -3), (1, 0), (1, -1), (1, -2), (1, -3))


def prepare_kernel(query_hbm, key_hbm, query_scales_hbm, key_scales_hbm, sent_ref, scales_ref, query_ref, key_ref, query_scales_ref, key_scales_ref, semaphores):
    moves = [
        pltpu.make_async_copy(source, to, semaphores.at[n])
        for n, (source, to) in enumerate(
            ((query_hbm, query_ref), (key_hbm, key_ref), (query_scales_hbm, query_scales_ref), (key_scales_hbm, key_scales_ref))
        )
    ]
    for move in moves:
        move.start()
    for move in moves:
        move.wait()
    for to in range(16):
        for layer in range(2):
            for rows_ref, start in ((query_ref, 0), (key_ref, 12)):
                rows = rows_ref.shape[1]
                tiles = rows_ref[layer, :, 8 * to : 8 * to + 8].reshape(8 * rows, 128)
                sent_ref[to, layer, 8 * start : 8 * (start + rows)] = tiles
    scales_ref[:, :12] = query_scales_ref[...].transpose(0, 2, 1)
    scales_ref[:, 12:] = key_scales_ref[...]


def prepare(query_codes, key_codes, query_scales, key_scales):
    args = (query_codes, key_codes, query_scales.transpose(0, 2, 1), key_scales)
    return pl.pallas_call(
        prepare_kernel,
        in_specs=[pl.BlockSpec(memory_space=pltpu.HBM)] * 4,
        out_specs=[pl.BlockSpec(memory_space=pltpu.VMEM)] * 2,
        out_shape=[
            jax.ShapeDtypeStruct((16, 2, 128, 128), jnp.bfloat16),
            jax.ShapeDtypeStruct((2, 16, 8), jnp.float32),
        ],
        scratch_shapes=[pltpu.VMEM(x.shape, x.dtype) for x in args] + [pltpu.SemaphoreType.DMA((4,))],
        compiler_params=pltpu.CompilerParams(vmem_limit_bytes=60 * 2**20),
        name="prepare",
    )(*args)


def regroup_matrix():
    to = lax.broadcasted_iota(jnp.int32, (256, 256), 0)
    head, place = to // 32, to % 32
    query = place < 24
    source = jnp.where(query, place // 12, (place - 24) // 4)
    row = jnp.where(query, place % 12, 12 + place % 4)
    start = source * 128 + row * 8 + head
    return (lax.broadcasted_iota(jnp.int32, (256, 256), 1) == start).astype(jnp.bfloat16)


def regroup_kernel(device_ref, scales_ref, dealt_ref, *out_refs):
    replica = device_ref[0] // 16
    matrix = regroup_matrix()
    for layer in range(2):
        codes = []
        for pair in range(8):
            rows = dealt_ref[2 * pair : 2 * pair + 2, layer].reshape(256, 128)
            codes.append(jnp.dot(matrix, rows, preferred_element_type=jnp.float32))
        for head in range(HEADS):
            unit = layer * HEADS + head
            out_ref, at = next((ref, unit - start) for ref, (start, end) in zip(out_refs, PARTS) if start <= unit < end)
            query = jnp.concatenate([c[32 * head : 32 * head + 24] for c in codes])
            for part in range(3):
                scale = scales_ref[layer, (3 * replica + part) // 2, head]
                out_ref[at, 64 * part : 64 * part + 64] = (query[64 * part : 64 * part + 64] * scale).astype(jnp.bfloat16)
            key = jnp.concatenate([c[32 * head + 24 : 32 * head + 32] for c in codes])
            scale = scales_ref[layer, 12 + replica // 2, head]
            out_ref[at, QROWS:] = (key * scale).astype(jnp.bfloat16)


def regroup(device, scales, dealt):
    smem, vmem = pl.BlockSpec(memory_space=pltpu.SMEM), pl.BlockSpec(memory_space=pltpu.VMEM)
    return pl.pallas_call(
        regroup_kernel,
        in_specs=[smem, smem, vmem],
        out_specs=[vmem] * len(PARTS),
        out_shape=[jax.ShapeDtypeStruct((end - start, ROWS, 128), jnp.bfloat16) for start, end in PARTS],
        compiler_params=pltpu.CompilerParams(vmem_limit_bytes=8 * 2**20),
        name="regroup",
    )(device, scales, dealt)


def absorb_kernel(device_ref, *refs):
    pieces, (out_ref, scale_ref, query_ref, key_ref, dots_ref, peak_ref) = refs[: len(PIECES)], refs[-6:]
    replica, core = device_ref[0] // 16, device_ref[0] % 2
    y, z, spin = replica // Z, replica % Z, 1 - 2 * core
    for (dy, dz), piece in zip(PIECES, pieces):
        place = (y + dy) % Y * Z + (z + Z + dz * spin) % Z
        query_ref[pl.ds(pl.multiple_of(QROWS * place, QROWS), QROWS)] = piece[0, :QROWS]
        key_ref[pl.ds(pl.multiple_of(KROWS * place, KROWS), KROWS)] = piece[0, QROWS:]

    def finish(i):
        rows = slice(BLK * i, BLK * (i + 1))
        for j in range(4):
            columns = slice(BLK * j, BLK * (j + 1))
            peak = jnp.max(peak_ref[i : i + 1, columns], axis=1, keepdims=True) + EPS
            scale_ref[0, 0, j : j + 1, i : i + 1] = peak
            out_ref[0, 0, rows, columns] = (dots_ref[rows, columns] * (1.0 / peak)).astype(jnp.bfloat16)

    for i in range(12):
        rows = slice(BLK * i, BLK * (i + 1))
        dots = lax.dot_general(query_ref[rows], key_ref[...], (((1,), (1,)), ((), ())), preferred_element_type=jnp.float32)
        dots_ref[rows] = dots
        peak_ref[i : i + 1] = jnp.max(jnp.abs(dots), axis=0, keepdims=True)
        if i:
            finish(i - 1)
    finish(11)


def absorb(device, part, pieces, outs):
    any_space = pl.BlockSpec(memory_space=pl.ANY)
    earlier = () if outs is None else tuple(outs)
    start, end = part
    return pl.pallas_call(
        absorb_kernel,
        grid_spec=pltpu.PrefetchScalarGridSpec(
            num_scalar_prefetch=1,
            grid=(end - start,),
            in_specs=[pl.BlockSpec((1, ROWS, 128), lambda u, device: (u, 0, 0))] * len(PIECES) + [any_space] * len(earlier),
            out_specs=[
                pl.BlockSpec((1, 1, 1536, 512), lambda u, device: ((start + u) // HEADS, (start + u) % HEADS, 0, 0)),
                pl.BlockSpec((1, 1, 4, 12), lambda u, device: ((start + u) // HEADS, (start + u) % HEADS, 0, 0)),
            ],
            scratch_shapes=[
                pltpu.VMEM((1536, 128), jnp.bfloat16),
                pltpu.VMEM((512, 128), jnp.bfloat16),
                pltpu.VMEM((1536, 512), jnp.float32),
                pltpu.VMEM((16, 512), jnp.float32),
            ],
        ),
        out_shape=[
            jax.ShapeDtypeStruct((2, HEADS, 1536, 512), jnp.bfloat16),
            jax.ShapeDtypeStruct((2, HEADS, 4, 12), jnp.float32),
        ],
        input_output_aliases={1 + len(pieces) + n: n for n in range(len(earlier))},
        compiler_params=pltpu.CompilerParams(vmem_limit_bytes=14 * 2**20),
        cost_estimate=pl.CostEstimate(flops=1, bytes_accessed=1, transcendentals=0),
        name="absorb",
    )(device, *pieces, *earlier)


def along_z(x, step):
    def to(replica, tensor):
        spin = 1 - 2 * (tensor % 2)
        return replica // Z * Z + (replica + step * spin) % Z

    pairs = [(16 * r + t, 16 * to(r, t) + t) for r in range(Y * Z) for t in range(16)]
    return lax.ppermute(x, ("replica", "tensor"), pairs)


def across_y(x):
    return lax.ppermute(x, "replica", [(y * Z + z, (1 - y) * Z + z) for y in range(Y) for z in range(Z)])


def together(*arrays):
    return lax.optimization_barrier(arrays)


def local(query_codes, key_codes, query_scales, key_scales):
    device = lax.axis_index(("replica", "tensor")).astype(jnp.int32).reshape(1)
    sent, scales = prepare(query_codes, key_codes, query_scales, key_scales)
    dealt = lax.all_to_all(sent, "tensor", split_axis=0, concat_axis=0, tiled=True)
    own = regroup(device, scales, dealt)

    own_0, own_1 = own
    outs = None
    a3_0 = along_z(own_0, -1)
    b3_0 = across_y(a3_0)
    a1_0 = along_z(own_0, 1)
    a2_0 = along_z(a1_0, 1)
    b0_0 = across_y(own_0)
    b0_1 = across_y(own_1)
    a1_1 = along_z(own_1, 1)
    a1_1, b0_0 = together(a1_1, b0_0)
    b1_0 = along_z(b0_0, 1)
    b2_0 = along_z(b1_0, 1)
    outs = absorb(device, PARTS[0], (own_0, a1_0, a2_0, a3_0, b0_0, b1_0, b2_0, b3_0), outs)
    b1_1 = across_y(a1_1)
    b2_1 = along_z(b1_1, 1)
    b3_1 = along_z(b2_1, 1)
    a2_1 = along_z(a1_1, 1)
    a3_1 = along_z(own_1, -1)
    outs = absorb(device, PARTS[1], (own_1, a1_1, a2_1, a3_1, b0_1, b1_1, b2_1, b3_1), outs)
    return outs[0], outs[1].transpose(0, 1, 3, 2)


def solution(mesh):
    return jax.shard_map(
        local,
        mesh=mesh,
        in_specs=(
            P(None, ("replica", "tensor"), None, None),
            P(None, ("replica", "tensor"), None, None),
            P(None, None, "tensor"),
            P(None, None, "tensor"),
        ),
        out_specs=(P(None, "tensor", None, None), P(None, "tensor", None, None)),
        check_vma=False,
    )
```

```python
import functools

import jax
import jax.numpy as jnp
from jax import lax
from jax.experimental import pallas as pl
from jax.experimental.pallas import tpu as pltpu
from jax.sharding import PartitionSpec as P

BLK = 128
EPS = 1e-06
QROWS = 192
KROWS = 64
ROWS = QROWS + KROWS
Z = 4
Y = 2
HEADS = 8
UNITS = 2 * HEADS
PARTS = ((0, 9), (9, 16))
PIECES = ((0, 0), (0, -1), (0, -2), (0, -3), (1, 0), (1, -1), (1, -2), (1, -3))


def prepare_kernel(query_hbm, key_hbm, query_scales_hbm, key_scales_hbm, sent_ref, scales_ref, query_ref, key_ref, query_scales_ref, key_scales_ref, semaphores):
    moves = [
        pltpu.make_async_copy(source, to, semaphores.at[n])
        for n, (source, to) in enumerate(
            ((query_hbm, query_ref), (key_hbm, key_ref), (query_scales_hbm, query_scales_ref), (key_scales_hbm, key_scales_ref))
        )
    ]
    for move in moves:
        move.start()
    for move in moves:
        move.wait()
    for to in range(16):
        for layer in range(2):
            for rows_ref, start in ((query_ref, 0), (key_ref, 12)):
                rows = rows_ref.shape[1]
                tiles = rows_ref[layer, :, 8 * to : 8 * to + 8].reshape(8 * rows, 128)
                sent_ref[to, layer, 8 * start : 8 * (start + rows)] = tiles
    scales_ref[:, :12] = query_scales_ref[...].transpose(0, 2, 1)
    scales_ref[:, 12:] = key_scales_ref[...]


def prepare(query_codes, key_codes, query_scales, key_scales):
    args = (query_codes, key_codes, query_scales.transpose(0, 2, 1), key_scales)
    return pl.pallas_call(
        prepare_kernel,
        in_specs=[pl.BlockSpec(memory_space=pltpu.HBM)] * 4,
        out_specs=[pl.BlockSpec(memory_space=pltpu.VMEM)] * 2,
        out_shape=[
            jax.ShapeDtypeStruct((16, 2, 128, 128), jnp.bfloat16),
            jax.ShapeDtypeStruct((2, 16, 8), jnp.float32),
        ],
        scratch_shapes=[pltpu.VMEM(x.shape, x.dtype) for x in args] + [pltpu.SemaphoreType.DMA((4,))],
        compiler_params=pltpu.CompilerParams(vmem_limit_bytes=60 * 2**20),
        name="prepare",
    )(*args)


def regroup_matrix():
    to = lax.broadcasted_iota(jnp.int32, (256, 256), 0)
    head, place = to // 32, to % 32
    query = place < 24
    source = jnp.where(query, place // 12, (place - 24) // 4)
    row = jnp.where(query, place % 12, 12 + place % 4)
    start = source * 128 + row * 8 + head
    return (lax.broadcasted_iota(jnp.int32, (256, 256), 1) == start).astype(jnp.bfloat16)


def regroup_kernel(device_ref, scales_ref, dealt_ref, *out_refs):
    replica = device_ref[0] // 16
    matrix = regroup_matrix()
    for layer in range(2):
        codes = []
        for pair in range(8):
            rows = dealt_ref[2 * pair : 2 * pair + 2, layer].reshape(256, 128)
            codes.append(jnp.dot(matrix, rows, preferred_element_type=jnp.float32))
        for head in range(HEADS):
            unit = layer * HEADS + head
            out_ref, at = next((ref, unit - start) for ref, (start, end) in zip(out_refs, PARTS) if start <= unit < end)
            query = jnp.concatenate([c[32 * head : 32 * head + 24] for c in codes])
            for part in range(3):
                scale = scales_ref[layer, (3 * replica + part) // 2, head]
                out_ref[at, 64 * part : 64 * part + 64] = (query[64 * part : 64 * part + 64] * scale).astype(jnp.bfloat16)
            key = jnp.concatenate([c[32 * head + 24 : 32 * head + 32] for c in codes])
            scale = scales_ref[layer, 12 + replica // 2, head]
            out_ref[at, QROWS:] = (key * scale).astype(jnp.bfloat16)


def regroup(device, scales, dealt):
    smem, vmem = pl.BlockSpec(memory_space=pltpu.SMEM), pl.BlockSpec(memory_space=pltpu.VMEM)
    return pl.pallas_call(
        regroup_kernel,
        in_specs=[smem, smem, vmem],
        out_specs=[vmem] * len(PARTS),
        out_shape=[jax.ShapeDtypeStruct((end - start, ROWS, 128), jnp.bfloat16) for start, end in PARTS],
        compiler_params=pltpu.CompilerParams(vmem_limit_bytes=8 * 2**20),
        name="regroup",
    )(device, scales, dealt)


def absorb_kernel(device_ref, *refs):
    pieces, (out_ref, scale_ref, query_ref, key_ref, dots_ref, peak_ref) = refs[: len(PIECES)], refs[-6:]
    replica, core = device_ref[0] // 16, device_ref[0] % 2
    y, z, spin = replica // Z, replica % Z, 1 - 2 * core
    for (dy, dz), piece in zip(PIECES, pieces):
        place = (y + dy) % Y * Z + (z + Z + dz * spin) % Z
        query_ref[pl.ds(pl.multiple_of(QROWS * place, QROWS), QROWS)] = piece[0, :QROWS]
        key_ref[pl.ds(pl.multiple_of(KROWS * place, KROWS), KROWS)] = piece[0, QROWS:]

    def finish(i):
        rows = slice(BLK * i, BLK * (i + 1))
        for j in range(4):
            columns = slice(BLK * j, BLK * (j + 1))
            peak = jnp.max(peak_ref[i : i + 1, columns], axis=1, keepdims=True) + EPS
            scale_ref[0, 0, j : j + 1, i : i + 1] = peak
            out_ref[0, 0, rows, columns] = (dots_ref[rows, columns] * (1.0 / peak)).astype(jnp.bfloat16)

    for i in range(12):
        rows = slice(BLK * i, BLK * (i + 1))
        dots = lax.dot_general(query_ref[rows], key_ref[...], (((1,), (1,)), ((), ())), preferred_element_type=jnp.float32)
        dots_ref[rows] = dots
        peak_ref[i : i + 1] = jnp.max(jnp.abs(dots), axis=0, keepdims=True)
        if i:
            finish(i - 1)
    finish(11)


def absorb(device, part, pieces, outs):
    any_space = pl.BlockSpec(memory_space=pl.ANY)
    earlier = () if outs is None else tuple(outs)
    start, end = part
    return pl.pallas_call(
        absorb_kernel,
        grid_spec=pltpu.PrefetchScalarGridSpec(
            num_scalar_prefetch=1,
            grid=(end - start,),
            in_specs=[pl.BlockSpec((1, ROWS, 128), lambda u, device: (u, 0, 0))] * len(PIECES) + [any_space] * len(earlier),
            out_specs=[
                pl.BlockSpec((1, 1, 1536, 512), lambda u, device: ((start + u) // HEADS, (start + u) % HEADS, 0, 0)),
                pl.BlockSpec((1, 1, 4, 12), lambda u, device: ((start + u) // HEADS, (start + u) % HEADS, 0, 0)),
            ],
            scratch_shapes=[
                pltpu.VMEM((1536, 128), jnp.bfloat16),
                pltpu.VMEM((512, 128), jnp.bfloat16),
                pltpu.VMEM((1536, 512), jnp.float32),
                pltpu.VMEM((16, 512), jnp.float32),
            ],
        ),
        out_shape=[
            jax.ShapeDtypeStruct((2, HEADS, 1536, 512), jnp.bfloat16),
            jax.ShapeDtypeStruct((2, HEADS, 4, 12), jnp.float32),
        ],
        input_output_aliases={1 + len(pieces) + n: n for n in range(len(earlier))},
        compiler_params=pltpu.CompilerParams(vmem_limit_bytes=14 * 2**20),
        cost_estimate=pl.CostEstimate(flops=1, bytes_accessed=1, transcendentals=0),
        name="absorb",
    )(device, *pieces, *earlier)


def along_z(x, step):
    def to(replica, tensor):
        spin = 1 - 2 * (tensor % 2)
        return replica // Z * Z + (replica + step * spin) % Z

    pairs = [(16 * r + t, 16 * to(r, t) + t) for r in range(Y * Z) for t in range(16)]
    return lax.ppermute(x, ("replica", "tensor"), pairs)


def across_y(x):
    return lax.ppermute(x, "replica", [(y * Z + z, (1 - y) * Z + z) for y in range(Y) for z in range(Z)])


def together(*arrays):
    return lax.optimization_barrier(arrays)


def local(query_codes, key_codes, query_scales, key_scales):
    device = lax.axis_index(("replica", "tensor")).astype(jnp.int32).reshape(1)
    sent, scales = prepare(query_codes, key_codes, query_scales, key_scales)
    dealt = lax.all_to_all(sent, "tensor", split_axis=0, concat_axis=0, tiled=True)
    own = regroup(device, scales, dealt)

    own_0, own_1 = own
    outs = None
    a3_1 = along_z(own_1, -1)
    b0_1 = across_y(own_1)
    a3_1, b0_1 = together(a3_1, b0_1)
    a1_1 = along_z(own_1, 1)
    a2_1 = along_z(a1_1, 1)
    a1_0 = along_z(own_0, 1)
    b3_1 = across_y(a3_1)
    b1_1 = along_z(b0_1, 1)
    b2_1 = along_z(b1_1, 1)
    b0_0 = across_y(own_0)
    a2_0 = along_z(a1_0, 1)
    b1_0 = along_z(b0_0, 1)
    b2_0 = along_z(b1_0, 1)
    a3_0 = along_z(own_0, -1)
    a2_0, a3_0 = together(a2_0, a3_0)
    b3_0 = across_y(a3_0)
    outs = absorb(device, PARTS[0], (own_0, a1_0, a2_0, a3_0, b0_0, b1_0, b2_0, b3_0), outs)
    outs = absorb(device, PARTS[1], (own_1, a1_1, a2_1, a3_1, b0_1, b1_1, b2_1, b3_1), outs)
    b2_1, *outs = together(b2_1, *outs)
    return outs[0], outs[1].transpose(0, 1, 3, 2)


def solution(mesh):
    return jax.shard_map(
        local,
        mesh=mesh,
        in_specs=(
            P(None, ("replica", "tensor"), None, None),
            P(None, ("replica", "tensor"), None, None),
            P(None, None, "tensor"),
            P(None, None, "tensor"),
        ),
        out_specs=(P(None, "tensor", None, None), P(None, "tensor", None, None)),
        check_vma=False,
    )
```

```python
import functools

import jax
import jax.numpy as jnp
from jax import lax
from jax.experimental import pallas as pl
from jax.experimental.pallas import tpu as pltpu
from jax.sharding import PartitionSpec as P

BLK = 128
EPS = 1e-06
QROWS = 192
KROWS = 64
ROWS = QROWS + KROWS
Z = 4
Y = 2
HEADS = 8
UNITS = 2 * HEADS
PARTS = ((0, 10), (10, 16))
PIECES = ((0, 0), (0, -1), (0, -2), (0, -3), (1, 0), (1, -1), (1, -2), (1, -3))


def prepare_kernel(query_hbm, key_hbm, query_scales_hbm, key_scales_hbm, sent_hbm, scales_ref, query_ref, key_ref, sent_ref, query_scales_ref, key_scales_ref, semaphores):
    def copy(n, source, to):
        return pltpu.make_async_copy(source, to, semaphores.at[n])

    codes_in = [
        (copy(2 * layer, query_hbm.at[layer], query_ref.at[layer]), copy(2 * layer + 1, key_hbm.at[layer], key_ref.at[layer]))
        for layer in range(2)
    ]
    scales_in = (copy(4, query_scales_hbm, query_scales_ref), copy(5, key_scales_hbm, key_scales_ref))
    out = [copy(6 + layer, sent_ref.at[:, layer], sent_hbm.at[:, layer]) for layer in range(2)]
    for move in (*codes_in[0], *codes_in[1], *scales_in):
        move.start()
    for layer in range(2):
        for move in codes_in[layer]:
            move.wait()
        for to in range(16):
            for rows_ref, start in ((query_ref, 0), (key_ref, 12)):
                rows = rows_ref.shape[1]
                tiles = rows_ref[layer, :, 8 * to : 8 * to + 8].reshape(8 * rows, 128)
                sent_ref[to, layer, 8 * start : 8 * (start + rows)] = tiles
        out[layer].start()
    for move in scales_in:
        move.wait()
    scales_ref[:, :12] = query_scales_ref[...].transpose(0, 2, 1)
    scales_ref[:, 12:] = key_scales_ref[...]
    for move in out:
        move.wait()


def prepare(query_codes, key_codes, query_scales, key_scales):
    query_scales = query_scales.transpose(0, 2, 1)
    args = (query_codes, key_codes, query_scales, key_scales)
    sent = jax.ShapeDtypeStruct((16, 2, 128, 128), jnp.bfloat16)
    return pl.pallas_call(
        prepare_kernel,
        in_specs=[pl.BlockSpec(memory_space=pltpu.HBM)] * 4,
        out_specs=[pl.BlockSpec(memory_space=pltpu.HBM), pl.BlockSpec(memory_space=pltpu.VMEM)],
        out_shape=[sent, jax.ShapeDtypeStruct((2, 16, 8), jnp.float32)],
        scratch_shapes=[pltpu.VMEM(x.shape, x.dtype) for x in (query_codes, key_codes, sent, query_scales, key_scales)]
        + [pltpu.SemaphoreType.DMA((8,))],
        compiler_params=pltpu.CompilerParams(vmem_limit_bytes=60 * 2**20),
        name="prepare",
    )(*args)


def regroup_matrix():
    to = lax.broadcasted_iota(jnp.int32, (256, 256), 0)
    head, place = to // 32, to % 32
    query = place < 24
    source = jnp.where(query, place // 12, (place - 24) // 4)
    row = jnp.where(query, place % 12, 12 + place % 4)
    start = source * 128 + row * 8 + head
    return (lax.broadcasted_iota(jnp.int32, (256, 256), 1) == start).astype(jnp.bfloat16)


def regroup_kernel(device_ref, scales_ref, dealt_ref, *out_refs):
    replica = device_ref[0] // 16
    matrix = regroup_matrix()
    for layer in range(2):
        codes = []
        for pair in range(8):
            rows = dealt_ref[2 * pair : 2 * pair + 2, layer].reshape(256, 128)
            codes.append(jnp.dot(matrix, rows, preferred_element_type=jnp.float32))
        for head in range(HEADS):
            unit = layer * HEADS + head
            out_ref, at = next((ref, unit - start) for ref, (start, end) in zip(out_refs, PARTS) if start <= unit < end)
            query = jnp.concatenate([c[32 * head : 32 * head + 24] for c in codes])
            for part in range(3):
                scale = scales_ref[layer, (3 * replica + part) // 2, head]
                out_ref[at, 64 * part : 64 * part + 64] = (query[64 * part : 64 * part + 64] * scale).astype(jnp.bfloat16)
            key = jnp.concatenate([c[32 * head + 24 : 32 * head + 32] for c in codes])
            scale = scales_ref[layer, 12 + replica // 2, head]
            out_ref[at, QROWS:] = (key * scale).astype(jnp.bfloat16)


def regroup(device, scales, dealt):
    smem, vmem = pl.BlockSpec(memory_space=pltpu.SMEM), pl.BlockSpec(memory_space=pltpu.VMEM)
    return pl.pallas_call(
        regroup_kernel,
        in_specs=[smem, smem, vmem],
        out_specs=[vmem] * len(PARTS),
        out_shape=[jax.ShapeDtypeStruct((end - start, ROWS, 128), jnp.bfloat16) for start, end in PARTS],
        compiler_params=pltpu.CompilerParams(vmem_limit_bytes=8 * 2**20),
        name="regroup",
    )(device, scales, dealt)


def absorb_kernel(device_ref, *refs):
    pieces, (out_ref, scale_ref, query_ref, key_ref, dots_ref, peak_ref) = refs[: len(PIECES)], refs[-6:]
    replica, core = device_ref[0] // 16, device_ref[0] % 2
    y, z, spin = replica // Z, replica % Z, 1 - 2 * core
    for (dy, dz), piece in zip(PIECES, pieces):
        place = (y + dy) % Y * Z + (z + Z + dz * spin) % Z
        query_ref[pl.ds(pl.multiple_of(QROWS * place, QROWS), QROWS)] = piece[0, :QROWS]
        key_ref[pl.ds(pl.multiple_of(KROWS * place, KROWS), KROWS)] = piece[0, QROWS:]

    def finish(i):
        rows = slice(BLK * i, BLK * (i + 1))
        for j in range(4):
            columns = slice(BLK * j, BLK * (j + 1))
            peak = jnp.max(peak_ref[i : i + 1, columns], axis=1, keepdims=True) + EPS
            scale_ref[0, 0, j : j + 1, i : i + 1] = peak
            out_ref[0, 0, rows, columns] = (dots_ref[rows, columns] * (1.0 / peak)).astype(jnp.bfloat16)

    for i in range(12):
        rows = slice(BLK * i, BLK * (i + 1))
        dots = lax.dot_general(query_ref[rows], key_ref[...], (((1,), (1,)), ((), ())), preferred_element_type=jnp.float32)
        dots_ref[rows] = dots
        peak_ref[i : i + 1] = jnp.max(jnp.abs(dots), axis=0, keepdims=True)
        if i:
            finish(i - 1)
    finish(11)


def absorb(device, part, pieces, outs):
    any_space = pl.BlockSpec(memory_space=pl.ANY)
    earlier = () if outs is None else tuple(outs)
    start, end = part
    return pl.pallas_call(
        absorb_kernel,
        grid_spec=pltpu.PrefetchScalarGridSpec(
            num_scalar_prefetch=1,
            grid=(end - start,),
            in_specs=[pl.BlockSpec((1, ROWS, 128), lambda u, device: (u, 0, 0))] * len(PIECES) + [any_space] * len(earlier),
            out_specs=[
                pl.BlockSpec((1, 1, 1536, 512), lambda u, device: ((start + u) // HEADS, (start + u) % HEADS, 0, 0)),
                pl.BlockSpec((1, 1, 4, 12), lambda u, device: ((start + u) // HEADS, (start + u) % HEADS, 0, 0)),
            ],
            scratch_shapes=[
                pltpu.VMEM((1536, 128), jnp.bfloat16),
                pltpu.VMEM((512, 128), jnp.bfloat16),
                pltpu.VMEM((1536, 512), jnp.float32),
                pltpu.VMEM((16, 512), jnp.float32),
            ],
        ),
        out_shape=[
            jax.ShapeDtypeStruct((2, HEADS, 1536, 512), jnp.bfloat16),
            jax.ShapeDtypeStruct((2, HEADS, 4, 12), jnp.float32),
        ],
        input_output_aliases={1 + len(pieces) + n: n for n in range(len(earlier))},
        compiler_params=pltpu.CompilerParams(vmem_limit_bytes=14 * 2**20),
        cost_estimate=pl.CostEstimate(flops=1, bytes_accessed=1, transcendentals=0),
        name="absorb",
    )(device, *pieces, *earlier)


def along_z(x, step):
    def to(replica, tensor):
        spin = 1 - 2 * (tensor % 2)
        return replica // Z * Z + (replica + step * spin) % Z

    pairs = [(16 * r + t, 16 * to(r, t) + t) for r in range(Y * Z) for t in range(16)]
    return lax.ppermute(x, ("replica", "tensor"), pairs)


def across_y(x):
    return lax.ppermute(x, "replica", [(y * Z + z, (1 - y) * Z + z) for y in range(Y) for z in range(Z)])


def together(*arrays):
    return lax.optimization_barrier(arrays)


def local(query_codes, key_codes, query_scales, key_scales):
    device = lax.axis_index(("replica", "tensor")).astype(jnp.int32).reshape(1)
    sent, scales = prepare(query_codes, key_codes, query_scales, key_scales)
    dealt = lax.all_to_all(sent, "tensor", split_axis=0, concat_axis=0, tiled=True)
    own = regroup(device, scales, dealt)

    own_0, own_1 = own
    outs = None
    a3_0 = along_z(own_0, -1)
    b3_0 = across_y(a3_0)
    a1_0 = along_z(own_0, 1)
    a2_0 = along_z(a1_0, 1)
    b0_0 = across_y(own_0)
    b0_1 = across_y(own_1)
    a1_1 = along_z(own_1, 1)
    a1_1, b0_0 = together(a1_1, b0_0)
    b1_0 = along_z(b0_0, 1)
    b2_0 = along_z(b1_0, 1)
    outs = absorb(device, PARTS[0], (own_0, a1_0, a2_0, a3_0, b0_0, b1_0, b2_0, b3_0), outs)
    b1_1 = across_y(a1_1)
    b2_1 = along_z(b1_1, 1)
    b3_1 = along_z(b2_1, 1)
    a2_1 = along_z(a1_1, 1)
    a3_1 = along_z(own_1, -1)
    outs = absorb(device, PARTS[1], (own_1, a1_1, a2_1, a3_1, b0_1, b1_1, b2_1, b3_1), outs)
    return outs[0], outs[1].transpose(0, 1, 3, 2)


def solution(mesh):
    return jax.shard_map(
        local,
        mesh=mesh,
        in_specs=(
            P(None, ("replica", "tensor"), None, None),
            P(None, ("replica", "tensor"), None, None),
            P(None, None, "tensor"),
            P(None, None, "tensor"),
        ),
        out_specs=(P(None, "tensor", None, None), P(None, "tensor", None, None)),
        check_vma=False,
    )
```
